32 devices in a mesh: row: 8 (over z, x), col: 4 (over y, core).
Axes of the slice: x: 2, y: 2, z: 4, core: 2. Of those that a mesh axis runs over, the one named last changes fastest.
Arguments:
- embeddings: bfloat16 [8192, 4096], P(('row', 'col')), as said below
- cluster_sizes: int32 [8], replicated, may hold values from 2 to 2048, as said below
Outputs:
- highest: float32 [8192], P(('row', 'col'))
The draws below stay inside these ranges and needn't reach their ends.
Inputs may be any that keep to these rules, and one draw needn't show every extreme that they name: `cluster_sizes`: 8 sizes summing to 8192; the largest is exactly 2048. `embeddings`: no row is zero.
All inputs are finite; a program needn't handle non-finite values.
Results may differ from the reference program's by a relative error of at most 0.00044.
Values may be sent and summed in bfloat16 or wider, within the bound.
No kernel may reach another device: no remote copies, remote signals or barrier semaphores. Data moves between devices by JAX's collectives and lax.ppermute only.
A program may use at most 128 MiB of HBM per device.

```python
import math
import jax
import jax.numpy as jnp
from jax import lax

D = 4096
ROWS_DEV = 256
SPAN = 8
ROWS = 8192
CLUSTERS = 8


def draw_embeddings(key, part):
    key = jax.random.fold_in(key, 11)
    subkeys = jax.random.split(key, 7)
    window = SPAN * ROWS_DEV
    groups = ROWS // window
    orders = jax.vmap(lambda single: jax.random.permutation(single, window))(jax.random.split(subkeys[0], groups))
    ranks = jnp.argsort(orders, axis=1, stable=True).astype(jnp.int32)
    partner = ((jnp.arange(groups, dtype=jnp.int32)[:, None] * window + ranks) // 2).reshape(ROWS)
    offset = jax.random.randint(subkeys[1], (), 0, ROWS, dtype=jnp.int32)
    partner = partner[(jnp.arange(ROWS, dtype=jnp.int32) + offset) % ROWS]
    shared = jax.random.normal(subkeys[2], (ROWS // 2, D), jnp.float32)
    strength = jnp.exp(jax.random.uniform(subkeys[3], (ROWS // 2,), jnp.float32, math.log(0.3), math.log(3.0)))
    noise = jax.random.normal(subkeys[4], (ROWS, D), jnp.float32)
    scales = jnp.exp(jax.random.uniform(subkeys[6], (ROWS,), jnp.float32, 0.0, math.log(10.0)))
    values = (strength[partner][:, None] * shared[partner] + noise) * scales[:, None]
    return values.astype(jnp.bfloat16)


def draw_cluster_sizes(key, part):
    key = jax.random.fold_in(key, 23)
    subkeys = jax.random.split(key, 2)
    largest = SPAN * ROWS_DEV
    remaining = ROWS - largest
    others = CLUSTERS - 1
    typical = remaining // others
    leftover = remaining - typical * others
    paired = others // 2
    offsets = jax.random.randint(subkeys[0], (paired,), -(typical - 2), typical - 1, dtype=jnp.int32)
    sizes = jnp.concatenate([jnp.full((1,), largest, jnp.int32), typical + offsets, typical - offsets, jnp.full((1,), typical + leftover, jnp.int32)])
    order = jax.random.permutation(subkeys[1], CLUSTERS)
    return sizes[order].astype(jnp.int32)


def setup_inputs(seed: int = 0) -> dict:
    splits = jax.random.split(jax.random.key(seed), 3)
    embeddings = draw_embeddings(jax.random.fold_in(splits[2], 71), 0)
    cluster_sizes = draw_cluster_sizes(jax.random.fold_in(splits[2], 71), 0)
    return {"embeddings": embeddings, "cluster_sizes": cluster_sizes}


def reference(embeddings, cluster_sizes):
    row_count = embeddings.shape[0]
    block = ROWS_DEV
    reach = SPAN * ROWS_DEV
    widened = embeddings.astype(jnp.float32)
    squares = lax.optimization_barrier(jnp.sum(widened * widened, axis=1, keepdims=True)) + 1e-06
    normed = (widened * lax.rsqrt(squares)).astype(jnp.bfloat16)
    bounds = jnp.cumsum(cluster_sizes).astype(jnp.int32)
    positions = jnp.arange(row_count, dtype=jnp.int32)
    labels = lax.optimization_barrier(jnp.sum((bounds[None, :] <= positions[:, None]).astype(jnp.int32), axis=1)).astype(jnp.int32)
    padding = jnp.zeros((reach, embeddings.shape[1]), jnp.bfloat16)
    padded = jnp.concatenate([padding, normed, padding], axis=0)
    fillers = jnp.full((reach,), -1, jnp.int32)
    padded_labels = jnp.concatenate([fillers, labels, fillers], axis=0)
    window = block + 2 * reach

    def one_block(index):
        start = (index * block).astype(jnp.int32)
        own_rows = lax.dynamic_slice_in_dim(normed, start, block, 0)
        own_labels = lax.dynamic_slice_in_dim(labels, start, block, 0)
        nearby = lax.dynamic_slice_in_dim(padded, start, window, 0)
        nearby_labels = lax.dynamic_slice_in_dim(padded_labels, start, window, 0)
        scores = lax.dot_general(own_rows, nearby, (((1,), (1,)), ((), ())), preferred_element_type=jnp.float32)
        own_index = jnp.arange(block, dtype=jnp.int32)[:, None] + reach
        near_index = jnp.arange(window, dtype=jnp.int32)[None, :]
        shared = (own_labels[:, None] == nearby_labels[None, :]) & (own_index != near_index)
        return lax.optimization_barrier(jnp.max(jnp.where(shared, scores, jnp.float32(-2.0)), axis=1))
    blocks = lax.map(one_block, jnp.arange(row_count // block, dtype=jnp.int32))
    return blocks.reshape(row_count)
```

```python
import functools

import jax
import jax.numpy as jnp
from jax import lax
from jax.experimental import pallas as pl
from jax.experimental.pallas import tpu as pltpu
from jax.sharding import PartitionSpec as P

AXES = ("row", "col")
QUAD = 4
STRIP = 16
FILLER = -2.0
NT = (((1,), (1,)), ((), ()))


def swapped(x, devices, bit):
    return lax.ppermute(x, AXES, [(i, i ^ bit) for i in range(devices)])


def shifted(x, devices, by):
    return lax.ppermute(x, AXES, [(i, i + by) for i in range(devices) if 0 <= i + by < devices])


def labels_of(bounds_ref, block, length, axis):
    shape = (length, 1) if axis == 0 else (1, length)
    positions = block * length + lax.broadcasted_iota(jnp.int32, shape, axis)
    labels = jnp.where(positions < 0, -1, 0)
    for c in range(bounds_ref.shape[0]):
        labels = labels + (bounds_ref[c] <= positions).astype(jnp.int32)
    return labels


def normalize(ref):
    def strip(i, unused):
        rows = pl.ds(pl.multiple_of(i * STRIP, STRIP), STRIP)
        widened = ref[rows, :].astype(jnp.float32)
        squares = jnp.sum(widened * widened, axis=1, keepdims=True) + 1e-06
        ref[rows, :] = (widened * lax.rsqrt(squares)).astype(jnp.bfloat16)
        return unused

    lax.fori_loop(0, ref.shape[0] // STRIP, strip, 0)


def masked_scores(left, right, left_labels, right_labels):
    scores = lax.dot_general(left[...], right[...], NT, preferred_element_type=jnp.float32)
    return jnp.where(left_labels == right_labels, scores, FILLER)


def over_lanes(masked):
    folded = masked[:, :128]
    for i in range(128, masked.shape[1], 128):
        folded = jnp.maximum(folded, masked[:, i:i + 128])
    return jnp.max(folded.T, axis=0, keepdims=True)


def chip_kernel(bounds_ref, place_ref, own_hbm, near_hbm, own_out, near_out, best_out, own, near, sems):
    length = own.shape[0]
    copies = [pltpu.make_async_copy(own_hbm, own, sems.at[0]), pltpu.make_async_copy(near_hbm, near, sems.at[1])]
    for copy in copies:
        copy.start()
    place = place_ref[0]
    own_labels = labels_of(bounds_ref, place, length, 1)
    copies[0].wait()
    normalize(own)
    back = [pltpu.make_async_copy(own, own_out, sems.at[2]), pltpu.make_async_copy(near, near_out, sems.at[3])]
    back[0].start()
    scores = masked_scores(own, own, labels_of(bounds_ref, place, length, 0), own_labels)
    same = lax.broadcasted_iota(jnp.int32, scores.shape, 0) == lax.broadcasted_iota(jnp.int32, scores.shape, 1)
    best = jnp.max(jnp.where(same, FILLER, scores), axis=0, keepdims=True)
    copies[1].wait()
    normalize(near)
    back[1].start()
    scores = masked_scores(near, own, labels_of(bounds_ref, place ^ 1, length, 0), own_labels)
    best_out[...] = jnp.maximum(best, jnp.max(scores, axis=0, keepdims=True))
    back[0].wait()
    back[1].wait()


def quad_kernel(bounds_ref, place_ref, *refs):
    sources, (best_in, best_out, quad_out, below_out, above_out), held, sems = refs[:6], refs[6:11], refs[11:17], refs[17]
    length = held[0].shape[0]
    copies = [pltpu.make_async_copy(sources[i], held[i], sems.at[i]) for i in range(6)]
    for i in (0, 1, 4, 5, 2, 3):
        copies[i].start()
    place = place_ref[0]
    quad_labels = [labels_of(bounds_ref, place ^ b, length, 1) for b in range(QUAD)]
    outside = (place - QUAD, place + 2 * QUAD)
    outside_labels = [labels_of(bounds_ref, block, length, 0) for block in outside]
    widest = [None, None]
    best = [None] * QUAD
    for b in range(QUAD):
        copies[b].wait()
        if b >= 2:
            normalize(held[b])
        for side in range(2):
            if b == 0:
                copies[4 + side].wait()
                normalize(held[4 + side])
            scores = masked_scores(held[4 + side], held[b], outside_labels[side], quad_labels[b])
            widest[side] = scores if b == 0 else jnp.maximum(widest[side], scores)
            found = jnp.max(scores, axis=0, keepdims=True)
            best[b] = found if side == 0 else jnp.maximum(best[b], found)
    for b in range(QUAD):
        quad_out[b:b + 1, :] = best[b]
    below_out[...] = over_lanes(widest[0])
    above_out[...] = over_lanes(widest[1])
    highest = best_in[...]
    for b in range(2, QUAD):
        scores = masked_scores(held[b], held[0], labels_of(bounds_ref, place ^ b, length, 0), quad_labels[0])
        highest = jnp.maximum(highest, jnp.max(scores, axis=0, keepdims=True))
    best_out[...] = highest


ANY = pl.BlockSpec(memory_space=pl.ANY)
VMEM = pl.BlockSpec(memory_space=pltpu.VMEM)
SMEM = pl.BlockSpec(memory_space=pltpu.SMEM)


def cost(products, blocks, length, width):
    return pl.CostEstimate(flops=2 * products * length * length * width, bytes_accessed=2 * blocks * length * width, transcendentals=0)


def local(devices, embeddings, cluster_sizes):
    length, width = embeddings.shape
    block = jax.ShapeDtypeStruct((length, width), jnp.bfloat16)
    line = jax.ShapeDtypeStruct((1, length), jnp.float32)
    place = lax.axis_index(AXES).astype(jnp.int32)
    bounds = jnp.cumsum(cluster_sizes).astype(jnp.int32)
    where = place.reshape(1)

    across = swapped(embeddings, devices, 2)
    below = shifted(embeddings, devices, QUAD)
    above = shifted(embeddings, devices, -2 * QUAD)
    near = swapped(embeddings, devices, 1)

    own_normed, near_normed, chip_best = pl.pallas_call(
        chip_kernel,
        out_shape=(block, block, line),
        in_specs=[SMEM, SMEM, ANY, ANY],
        out_specs=(ANY, ANY, VMEM),
        scratch_shapes=[pltpu.VMEM((length, width), jnp.bfloat16)] * 2 + [pltpu.SemaphoreType.DMA((4,))],
        compiler_params=pltpu.CompilerParams(vmem_limit_bytes=16 << 20),
        cost_estimate=cost(2, 4, length, width),
    )(bounds, where, embeddings, near)

    across_near = swapped(across, devices, 1)

    best, quad, to_below, to_above = pl.pallas_call(
        quad_kernel,
        out_shape=(line, jax.ShapeDtypeStruct((QUAD, length), jnp.float32), line, line),
        in_specs=[SMEM, SMEM] + [ANY] * 6 + [VMEM],
        out_specs=(VMEM,) * 4,
        scratch_shapes=[pltpu.VMEM((length, width), jnp.bfloat16)] * 6 + [pltpu.SemaphoreType.DMA((6,))],
        compiler_params=pltpu.CompilerParams(vmem_limit_bytes=24 << 20),
        cost_estimate=cost(10, 6, length, width),
    )(bounds, where, own_normed, near_normed, across, across_near, below, above, chip_best)

    filler = jnp.float32(FILLER)
    from_next = shifted(to_below, devices, -QUAD)
    from_previous = shifted(to_above, devices, 2 * QUAD)
    swapped_chip = swapped(quad[1::2], devices, 1)
    own_chip = jnp.maximum(quad[0::2], swapped_chip)
    swapped_quad = swapped(own_chip[1:2], devices, 2)
    best = jnp.maximum(jnp.maximum(best, own_chip[0:1]), swapped_quad)
    best = jnp.maximum(best, jnp.where(place + QUAD < devices, from_next, filler))
    best = jnp.maximum(best, jnp.where(place >= 2 * QUAD, from_previous, filler))
    return best.reshape(length)


def solution(mesh):
    devices = 1
    for axis in AXES:
        devices *= mesh.shape[axis]
    in_specs = (P(AXES, None), P())
    return jax.shard_map(functools.partial(local, devices), mesh=mesh, in_specs=in_specs, out_specs=P(AXES), check_vma=False)
```

```python
import functools

import jax
import jax.numpy as jnp
from jax import lax
from jax.experimental import pallas as pl
from jax.experimental.pallas import tpu as pltpu
from jax.sharding import PartitionSpec as P

AXES = ("row", "col")
QUAD = 4
STRIP = 16
FILLER = -2.0
NT = (((1,), (1,)), ((), ()))


def swapped(x, devices, bit):
    return lax.ppermute(x, AXES, [(i, i ^ bit) for i in range(devices)])


def shifted(x, devices, by):
    return lax.ppermute(x, AXES, [(i, i + by) for i in range(devices) if 0 <= i + by < devices])


def labels_of(bounds_ref, block, length, axis):
    shape = (length, 1) if axis == 0 else (1, length)
    positions = block * length + lax.broadcasted_iota(jnp.int32, shape, axis)
    labels = jnp.where(positions < 0, -1, 0)
    for c in range(bounds_ref.shape[0]):
        labels = labels + (bounds_ref[c] <= positions).astype(jnp.int32)
    return labels


def label_at(bounds_ref, row):
    label = jnp.where(row < 0, -1, 0)
    for c in range(bounds_ref.shape[0]):
        label = label + jnp.where(bounds_ref[c] <= row, 1, 0)
    return label


def touch(bounds_ref, one, other, length):
    lower, upper = jnp.minimum(one, other), jnp.maximum(one, other)
    return label_at(bounds_ref, (lower + 1) * length - 1) == label_at(bounds_ref, upper * length)


def masked_scores(left, right, left_labels, right_labels):
    scores = lax.dot_general(left[...], right[...], NT, preferred_element_type=jnp.float32)
    return jnp.where(left_labels == right_labels, scores, FILLER)


def folded(masked):
    result = masked[:, :128]
    for i in range(128, masked.shape[1], 128):
        result = jnp.maximum(result, masked[:, i:i + 128])
    return result


def over_rows(masked):
    return jnp.max(masked, axis=0, keepdims=True)


def normalize_kernel(raw_hbm, normed_hbm, raw, normed, in_sems, out_sems):
    pieces = in_sems.shape[0]
    length = raw.shape[0] // pieces
    incoming, outgoing = [], []
    for i in range(pieces):
        rows = pl.ds(i * length, length)
        incoming.append(pltpu.make_async_copy(raw_hbm.at[rows], raw.at[rows], in_sems.at[i]))
        outgoing.append(pltpu.make_async_copy(normed.at[rows], normed_hbm.at[rows], out_sems.at[i]))
    for copy in incoming:
        copy.start()
    for i in range(pieces):
        incoming[i].wait()
        for j in range(0, length, STRIP):
            rows = pl.ds(i * length + j, STRIP)
            widened = raw[rows, :].astype(jnp.float32)
            squares = jnp.sum(widened * widened, axis=1, keepdims=True) + 1e-06
            normed[rows, :] = (widened * lax.rsqrt(squares)).astype(jnp.bfloat16)
        outgoing[i].start()
    for copy in outgoing:
        copy.wait()


def chip_kernel(bounds_ref, place_ref, own_hbm, near_hbm, best_out, own, near, sems):
    length = own.shape[0]
    copies = [pltpu.make_async_copy(own_hbm, own, sems.at[0]), pltpu.make_async_copy(near_hbm, near, sems.at[1])]
    for copy in copies:
        copy.start()
    place = place_ref[0]
    own_labels = labels_of(bounds_ref, place, length, 1)
    copies[0].wait()
    scores = masked_scores(own, own, labels_of(bounds_ref, place, length, 0), own_labels)
    same = lax.broadcasted_iota(jnp.int32, scores.shape, 0) == lax.broadcasted_iota(jnp.int32, scores.shape, 1)
    best = over_rows(jnp.where(same, FILLER, scores))
    copies[1].wait()
    scores = masked_scores(near, own, labels_of(bounds_ref, place ^ 1, length, 0), own_labels)
    best_out[...] = jnp.maximum(best, over_rows(scores))


def quad_kernel(bounds_ref, place_ref, *refs):
    sources, (best_in, best_out, quad_out, below_out, above_out), held, (widest, sems) = refs[:6], refs[6:11], refs[11:17], refs[17:]
    length = held[0].shape[0]
    copies = [pltpu.make_async_copy(sources[i], held[i], sems.at[i]) for i in range(6)]
    for i in (4, 0, 1, 5, 2, 3):
        copies[i].start()
    place = place_ref[0]
    outside = (place - QUAD, place + 2 * QUAD)
    outside_labels = [labels_of(bounds_ref, block, length, 0) for block in outside]
    widest[...] = jnp.full_like(widest, FILLER)
    quad_out[...] = jnp.full_like(quad_out, FILLER)
    best_out[...] = best_in[...]
    for b in range(QUAD):
        block = place ^ b
        block_labels = labels_of(bounds_ref, block, length, 1)
        for side in range(2):
            if b == 0:
                copies[4 + side].wait()
            if side == 0:
                copies[b].wait()

            @pl.when(touch(bounds_ref, block, outside[side], length))
            def _():
                scores = masked_scores(held[4 + side], held[b], outside_labels[side], block_labels)
                widest[side] = jnp.maximum(widest[side], folded(scores))
                quad_out[b:b + 1, :] = jnp.maximum(quad_out[b:b + 1, :], over_rows(scores))

        if b >= 2:

            @pl.when(touch(bounds_ref, block, place, length))
            def _():
                own_labels = labels_of(bounds_ref, place, length, 1)
                scores = masked_scores(held[b], held[0], labels_of(bounds_ref, block, length, 0), own_labels)
                best_out[...] = jnp.maximum(best_out[...], over_rows(scores))

    below_out[...] = over_rows(widest[0].T)
    above_out[...] = over_rows(widest[1].T)


ANY = pl.BlockSpec(memory_space=pl.ANY)
VMEM = pl.BlockSpec(memory_space=pltpu.VMEM)
SMEM = pl.BlockSpec(memory_space=pltpu.SMEM)


def cost(products, blocks, length, width):
    return pl.CostEstimate(flops=2 * products * length * length * width, bytes_accessed=2 * blocks * length * width, transcendentals=0)


def local(devices, embeddings, cluster_sizes):
    length, width = embeddings.shape
    block = jax.ShapeDtypeStruct((length, width), jnp.bfloat16)
    line = jax.ShapeDtypeStruct((1, length), jnp.float32)
    place = lax.axis_index(AXES).astype(jnp.int32)
    bounds = jnp.cumsum(cluster_sizes).astype(jnp.int32)
    where = place.reshape(1)

    normed = pl.pallas_call(
        normalize_kernel,
        out_shape=block,
        in_specs=[ANY],
        out_specs=ANY,
        scratch_shapes=[pltpu.VMEM((length, width), jnp.bfloat16)] * 2 + [pltpu.SemaphoreType.DMA((4,))] * 2,
        compiler_params=pltpu.CompilerParams(vmem_limit_bytes=60 << 20),
        cost_estimate=cost(0, 2, length, width),
    )(embeddings)

    across = swapped(normed, devices, 2)
    below = shifted(normed, devices, QUAD)
    above = shifted(normed, devices, -2 * QUAD)
    near = swapped(normed, devices, 1)

    chip_best = pl.pallas_call(
        chip_kernel,
        out_shape=line,
        in_specs=[SMEM, SMEM, ANY, ANY],
        out_specs=VMEM,
        scratch_shapes=[pltpu.VMEM((length, width), jnp.bfloat16)] * 2 + [pltpu.SemaphoreType.DMA((2,))],
        compiler_params=pltpu.CompilerParams(vmem_limit_bytes=24 << 20),
        cost_estimate=cost(2, 4, length, width),
    )(bounds, where, normed, near)

    across, chip_best = lax.optimization_barrier((across, chip_best))
    across_near = swapped(across, devices, 1)

    best, quad, to_below, to_above = pl.pallas_call(
        quad_kernel,
        out_shape=(line, jax.ShapeDtypeStruct((QUAD, length), jnp.float32), line, line),
        in_specs=[SMEM, SMEM] + [ANY] * 6 + [VMEM],
        out_specs=(VMEM,) * 4,
        scratch_shapes=[pltpu.VMEM((length, width), jnp.bfloat16)] * 6
        + [pltpu.VMEM((2, length, 128), jnp.float32), pltpu.SemaphoreType.DMA((6,))],
        compiler_params=pltpu.CompilerParams(vmem_limit_bytes=32 << 20),
        cost_estimate=cost(10, 6, length, width),
    )(bounds, where, normed, near, across, across_near, below, above, chip_best)

    filler = jnp.float32(FILLER)
    from_next = shifted(to_below, devices, -QUAD)
    from_previous = shifted(to_above, devices, 2 * QUAD)
    swapped_chip = swapped(quad[1::2], devices, 1)
    own_chip = jnp.maximum(quad[0::2], swapped_chip)
    swapped_quad = swapped(own_chip[1:2], devices, 2)
    best = jnp.maximum(jnp.maximum(best, own_chip[0:1]), swapped_quad)
    best = jnp.maximum(best, jnp.where(place + QUAD < devices, from_next, filler))
    best = jnp.maximum(best, jnp.where(place >= 2 * QUAD, from_previous, filler))
    return best.reshape(length)


def solution(mesh):
    devices = 1
    for axis in AXES:
        devices *= mesh.shape[axis]
    in_specs = (P(AXES, None), P())
    return jax.shard_map(functools.partial(local, devices), mesh=mesh, in_specs=in_specs, out_specs=P(AXES), check_vma=False)
```

```python
import functools

import jax
import jax.numpy as jnp
from jax import lax
from jax.experimental import pallas as pl
from jax.experimental.pallas import tpu as pltpu
from jax.sharding import PartitionSpec as P

AXES = ("row", "col")
QUAD = 4
STRIP = 16
FILLER = -2.0
NT = (((1,), (1,)), ((), ()))


def swapped(x, devices, bit):
    return lax.ppermute(x, AXES, [(i, i ^ bit) for i in range(devices)])


def shifted(x, devices, even, odd):
    moves = [(i, i + (odd if i % 2 else even)) for i in range(devices)]
    return lax.ppermute(x, AXES, [(i, j) for i, j in moves if 0 <= j < devices])


def labels_of(bounds_ref, block, length, axis):
    shape = (length, 1) if axis == 0 else (1, length)
    positions = block * length + lax.broadcasted_iota(jnp.int32, shape, axis)
    labels = jnp.where(positions < 0, -1, 0)
    for c in range(bounds_ref.shape[0]):
        labels = labels + (bounds_ref[c] <= positions).astype(jnp.int32)
    return labels


def label_at(bounds_ref, row):
    label = jnp.where(row < 0, -1, 0)
    for c in range(bounds_ref.shape[0]):
        label = label + jnp.where(bounds_ref[c] <= row, 1, 0)
    return label


def touch(bounds_ref, one, other, length):
    lower, upper = jnp.minimum(one, other), jnp.maximum(one, other)
    return label_at(bounds_ref, (lower + 1) * length - 1) == label_at(bounds_ref, upper * length)


def masked_scores(left, right, left_labels, right_labels):
    scores = lax.dot_general(left[...], right[...], NT, preferred_element_type=jnp.float32)
    return jnp.where(left_labels == right_labels, scores, FILLER)


def folded(masked):
    result = masked[:, :128]
    for i in range(128, masked.shape[1], 128):
        result = jnp.maximum(result, masked[:, i:i + 128])
    return result


def over_rows(masked):
    return jnp.max(masked, axis=0, keepdims=True)


def normalize_kernel(raw_hbm, normed_hbm, raw, normed, in_sems, out_sems):
    pieces = in_sems.shape[0]
    length = raw.shape[0] // pieces
    incoming, outgoing = [], []
    for i in range(pieces):
        rows = pl.ds(i * length, length)
        incoming.append(pltpu.make_async_copy(raw_hbm.at[rows], raw.at[rows], in_sems.at[i]))
        outgoing.append(pltpu.make_async_copy(normed.at[rows], normed_hbm.at[rows], out_sems.at[i]))
    for copy in incoming:
        copy.start()
    for i in range(pieces):
        incoming[i].wait()
        for j in range(0, length, STRIP):
            rows = pl.ds(i * length + j, STRIP)
            widened = raw[rows, :].astype(jnp.float32)
            squares = jnp.sum(widened * widened, axis=1, keepdims=True) + 1e-06
            normed[rows, :] = (widened * lax.rsqrt(squares)).astype(jnp.bfloat16)
        outgoing[i].start()
    for copy in outgoing:
        copy.wait()


def chip_kernel(bounds_ref, place_ref, own_hbm, near_hbm, best_out, own, near, sems):
    length = own.shape[0]
    copies = [pltpu.make_async_copy(own_hbm, own, sems.at[0]), pltpu.make_async_copy(near_hbm, near, sems.at[1])]
    for copy in copies:
        copy.start()
    place = place_ref[0]
    own_labels = labels_of(bounds_ref, place, length, 1)
    copies[0].wait()
    scores = masked_scores(own, own, labels_of(bounds_ref, place, length, 0), own_labels)
    same = lax.broadcasted_iota(jnp.int32, scores.shape, 0) == lax.broadcasted_iota(jnp.int32, scores.shape, 1)
    best = over_rows(jnp.where(same, FILLER, scores))
    copies[1].wait()
    scores = masked_scores(near, own, labels_of(bounds_ref, place ^ 1, length, 0), own_labels)
    best_out[...] = jnp.maximum(best, over_rows(scores))


def quad_kernel(bounds_ref, place_ref, *refs):
    sources, (best_in, best_out, quad_out, first_out, second_out), held, (widest, sems) = refs[:6], refs[6:11], refs[11:17], refs[17:]
    length = held[0].shape[0]
    copies = [pltpu.make_async_copy(sources[i], held[i], sems.at[i]) for i in range(6)]
    for i in (4, 0, 1, 5, 2, 3):
        copies[i].start()
    place = place_ref[0]
    below, above = place - QUAD, place + 2 * QUAD
    even = place % 2 == 0
    outside = (jnp.where(even, below, above), jnp.where(even, above, below))
    outside_labels = [labels_of(bounds_ref, block, length, 0) for block in outside]
    widest[...] = jnp.full_like(widest, FILLER)
    quad_out[...] = jnp.full_like(quad_out, FILLER)
    best_out[...] = best_in[...]
    for b in range(QUAD):
        block = place ^ b
        block_labels = labels_of(bounds_ref, block, length, 1)
        for side in range(2):
            if b == 0:
                copies[4 + side].wait()
            if side == 0:
                copies[b].wait()

            @pl.when(touch(bounds_ref, block, outside[side], length))
            def _():
                scores = masked_scores(held[4 + side], held[b], outside_labels[side], block_labels)
                widest[side] = jnp.maximum(widest[side], folded(scores))
                quad_out[b:b + 1, :] = jnp.maximum(quad_out[b:b + 1, :], over_rows(scores))

        if b >= 2:

            @pl.when(touch(bounds_ref, block, place, length))
            def _():
                own_labels = labels_of(bounds_ref, place, length, 1)
                scores = masked_scores(held[b], held[0], labels_of(bounds_ref, block, length, 0), own_labels)
                best_out[...] = jnp.maximum(best_out[...], over_rows(scores))

    first_out[...] = over_rows(widest[0].T)
    second_out[...] = over_rows(widest[1].T)


ANY = pl.BlockSpec(memory_space=pl.ANY)
VMEM = pl.BlockSpec(memory_space=pltpu.VMEM)
SMEM = pl.BlockSpec(memory_space=pltpu.SMEM)


def cost(products, blocks, length, width):
    return pl.CostEstimate(flops=2 * products * length * length * width, bytes_accessed=2 * blocks * length * width, transcendentals=0)


def local(devices, embeddings, cluster_sizes):
    length, width = embeddings.shape
    block = jax.ShapeDtypeStruct((length, width), jnp.bfloat16)
    line = jax.ShapeDtypeStruct((1, length), jnp.float32)
    place = lax.axis_index(AXES).astype(jnp.int32)
    bounds = jnp.cumsum(cluster_sizes).astype(jnp.int32)
    where = place.reshape(1)

    normed = pl.pallas_call(
        normalize_kernel,
        out_shape=block,
        in_specs=[ANY],
        out_specs=ANY,
        scratch_shapes=[pltpu.VMEM((length, width), jnp.bfloat16)] * 2 + [pltpu.SemaphoreType.DMA((4,))] * 2,
        compiler_params=pltpu.CompilerParams(vmem_limit_bytes=60 << 20),
        cost_estimate=cost(0, 2, length, width),
    )(embeddings)

    across = swapped(normed, devices, 2)
    first = shifted(normed, devices, QUAD, -2 * QUAD)
    second = shifted(normed, devices, -2 * QUAD, QUAD)

    near = swapped(normed, devices, 1)

    chip_best = pl.pallas_call(
        chip_kernel,
        out_shape=line,
        in_specs=[SMEM, SMEM, ANY, ANY],
        out_specs=VMEM,
        scratch_shapes=[pltpu.VMEM((length, width), jnp.bfloat16)] * 2 + [pltpu.SemaphoreType.DMA((2,))],
        compiler_params=pltpu.CompilerParams(vmem_limit_bytes=24 << 20),
        cost_estimate=cost(2, 4, length, width),
    )(bounds, where, normed, near)

    across, chip_best = lax.optimization_barrier((across, chip_best))
    across_near = swapped(across, devices, 1)

    best, quad, first_best, second_best = pl.pallas_call(
        quad_kernel,
        out_shape=(line, jax.ShapeDtypeStruct((QUAD, length), jnp.float32), line, line),
        in_specs=[SMEM, SMEM] + [ANY] * 6 + [VMEM],
        out_specs=(VMEM,) * 4,
        scratch_shapes=[pltpu.VMEM((length, width), jnp.bfloat16)] * 6
        + [pltpu.VMEM((2, length, 128), jnp.float32), pltpu.SemaphoreType.DMA((6,))],
        compiler_params=pltpu.CompilerParams(vmem_limit_bytes=32 << 20),
        cost_estimate=cost(10, 6, length, width),
    )(bounds, where, normed, near, across, across_near, first, second, chip_best)

    swapped_chip = swapped(quad[1::2], devices, 1)
    first_back = shifted(first_best, devices, -QUAD, 2 * QUAD)
    second_back = shifted(second_best, devices, 2 * QUAD, -QUAD)
    own_chip = jnp.maximum(quad[0::2], swapped_chip)
    swapped_quad = swapped(own_chip[1:2], devices, 2)
    best = jnp.maximum(jnp.maximum(best, own_chip[0:1]), swapped_quad)
    even = place % 2 == 0
    from_next, from_previous = place + QUAD < devices, place >= 2 * QUAD
    filler = jnp.float32(FILLER)
    best = jnp.maximum(best, jnp.where(jnp.where(even, from_next, from_previous), first_back, filler))
    best = jnp.maximum(best, jnp.where(jnp.where(even, from_previous, from_next), second_back, filler))
    return best.reshape(length)


def solution(mesh):
    devices = 1
    for axis in AXES:
        devices *= mesh.shape[axis]
    in_specs = (P(AXES, None), P())
    return jax.shard_map(functools.partial(local, devices), mesh=mesh, in_specs=in_specs, out_specs=P(AXES), check_vma=False)
```

```python
import functools

import jax
import jax.numpy as jnp
from jax import lax
from jax.experimental import pallas as pl
from jax.experimental.pallas import tpu as pltpu
from jax.sharding import PartitionSpec as P

AXES = ("row", "col")
QUAD = 4
STRIP = 16
FILLER = -2.0
IN_QUAD = ("own", "near", "across", "across_near")
NT = (((1,), (1,)), ((), ()))


def swapped(x, devices, bit):
    return lax.ppermute(x, AXES, [(i, i ^ bit) for i in range(devices)])


def shifted(x, devices, even, odd):
    moves = [(i, i + (odd if i % 2 else even)) for i in range(devices)]
    return lax.ppermute(x, AXES, [(i, j) for i, j in moves if 0 <= j < devices])


def labels_of(bounds_ref, block, length, axis):
    shape = (length, 1) if axis == 0 else (1, length)
    positions = block * length + lax.broadcasted_iota(jnp.int32, shape, axis)
    labels = jnp.where(positions < 0, -1, 0)
    for c in range(bounds_ref.shape[0]):
        labels = labels + (bounds_ref[c] <= positions).astype(jnp.int32)
    return labels


def label_at(bounds_ref, row):
    label = jnp.where(row < 0, -1, 0)
    for c in range(bounds_ref.shape[0]):
        label = label + jnp.where(bounds_ref[c] <= row, 1, 0)
    return label


def touch(bounds_ref, one, other, length):
    lower, upper = jnp.minimum(one, other), jnp.maximum(one, other)
    return label_at(bounds_ref, (lower + 1) * length - 1) == label_at(bounds_ref, upper * length)


def masked_scores(left, right, left_labels, right_labels):
    scores = lax.dot_general(left[...], right[...], NT, preferred_element_type=jnp.float32)
    return jnp.where(left_labels == right_labels, scores, FILLER)


def folded(masked):
    result = masked[:, :128]
    for i in range(128, masked.shape[1], 128):
        result = jnp.maximum(result, masked[:, i:i + 128])
    return result


def over_rows(masked):
    return jnp.max(masked, axis=0, keepdims=True)


def normalize_kernel(raw_hbm, normed_hbm, raw, normed, in_sems, out_sems):
    pieces = in_sems.shape[0]
    length = raw.shape[0] // pieces
    incoming, outgoing = [], []
    for i in range(pieces):
        rows = pl.ds(i * length, length)
        incoming.append(pltpu.make_async_copy(raw_hbm.at[rows], raw.at[rows], in_sems.at[i]))
        outgoing.append(pltpu.make_async_copy(normed.at[rows], normed_hbm.at[rows], out_sems.at[i]))
    for copy in incoming:
        copy.start()
    for i in range(pieces):
        incoming[i].wait()
        for j in range(0, length, STRIP):
            rows = pl.ds(i * length + j, STRIP)
            widened = raw[rows, :].astype(jnp.float32)
            squares = jnp.sum(widened * widened, axis=1, keepdims=True) + 1e-06
            normed[rows, :] = (widened * lax.rsqrt(squares)).astype(jnp.bfloat16)
        outgoing[i].start()
    for copy in outgoing:
        copy.wait()


def products_kernel(names, pairs, starts, ends, bounds_ref, place_ref, *refs):
    sources, refs = refs[:len(names)], refs[len(names):]
    if not starts:
        entering, refs = refs[:3], refs[3:]
    (quad_out, first_out, second_out), held, refs = refs[:3], refs[3:3 + len(names)], refs[3 + len(names):]
    widest = dict(zip(("first", "second"), refs[:2] if ends else (first_out, second_out)))
    sems = refs[-1]
    length = held[0].shape[0]
    copies = [pltpu.make_async_copy(sources[i], held[i], sems.at[i]) for i in range(len(names))]
    for copy in copies:
        copy.start()
    for i, ref in enumerate((quad_out, widest["first"], widest["second"])):
        ref[...] = jnp.full_like(ref, FILLER) if starts else entering[i][...]
    place = place_ref[0]
    below, above = place - QUAD, place + 2 * QUAD
    even = place % 2 == 0
    blocks = {name: place ^ b for b, name in enumerate(IN_QUAD)}
    blocks["first"], blocks["second"] = jnp.where(even, below, above), jnp.where(even, above, below)
    landed = set()
    for left, right in pairs:
        for name in (left, right):
            if name not in landed:
                copies[names.index(name)].wait()
                landed.add(name)

        def multiply(left=left, right=right):
            left_labels = labels_of(bounds_ref, blocks[left], length, 0)
            right_labels = labels_of(bounds_ref, blocks[right], length, 1)
            scores = masked_scores(held[names.index(left)], held[names.index(right)], left_labels, right_labels)
            if left == right:
                rows = lax.broadcasted_iota(jnp.int32, scores.shape, 0)
                columns = lax.broadcasted_iota(jnp.int32, scores.shape, 1)
                scores = jnp.where(rows == columns, FILLER, scores)
            b = IN_QUAD.index(right)
            quad_out[b:b + 1, :] = jnp.maximum(quad_out[b:b + 1, :], over_rows(scores))
            if left in widest:
                widest[left][...] = jnp.maximum(widest[left][...], folded(scores))

        if left == right:
            multiply()
        else:
            pl.when(touch(bounds_ref, blocks[left], blocks[right], length))(multiply)
    if ends:
        first_out[...] = over_rows(widest["first"][...].T)
        second_out[...] = over_rows(widest["second"][...].T)


ANY = pl.BlockSpec(memory_space=pl.ANY)
VMEM = pl.BlockSpec(memory_space=pltpu.VMEM)
SMEM = pl.BlockSpec(memory_space=pltpu.SMEM)


def products(bounds, where, blocks, pairs, state=None, ends=False):
    names = tuple(blocks)
    length, width = blocks[names[0]].shape
    folds = jax.ShapeDtypeStruct((length, 128), jnp.float32)
    line = jax.ShapeDtypeStruct((1, length), jnp.float32)
    scratch = [pltpu.VMEM((length, width), jnp.bfloat16)] * len(names)
    if ends:
        scratch += [pltpu.VMEM((length, 128), jnp.float32)] * 2
    entering = () if state is None else state
    return pl.pallas_call(
        functools.partial(products_kernel, names, pairs, state is None, ends),
        out_shape=(jax.ShapeDtypeStruct((QUAD, length), jnp.float32),) + ((line, line) if ends else (folds, folds)),
        in_specs=[SMEM, SMEM] + [ANY] * len(names) + [VMEM] * len(entering),
        out_specs=(VMEM,) * 3,
        scratch_shapes=scratch + [pltpu.SemaphoreType.DMA((len(names),))],
        compiler_params=pltpu.CompilerParams(vmem_limit_bytes=24 << 20),
        cost_estimate=pl.CostEstimate(
            flops=2 * len(pairs) * length * length * width,
            bytes_accessed=2 * len(names) * length * width,
            transcendentals=0,
        ),
    )(bounds, where, *blocks.values(), *entering)


def local(devices, embeddings, cluster_sizes):
    length, width = embeddings.shape
    block = jax.ShapeDtypeStruct((length, width), jnp.bfloat16)
    place = lax.axis_index(AXES).astype(jnp.int32)
    bounds = jnp.cumsum(cluster_sizes).astype(jnp.int32)
    where = place.reshape(1)

    normed = pl.pallas_call(
        normalize_kernel,
        out_shape=block,
        in_specs=[ANY],
        out_specs=ANY,
        scratch_shapes=[pltpu.VMEM((length, width), jnp.bfloat16)] * 2 + [pltpu.SemaphoreType.DMA((4,))] * 2,
        compiler_params=pltpu.CompilerParams(vmem_limit_bytes=60 << 20),
        cost_estimate=pl.CostEstimate(flops=0, bytes_accessed=4 * length * width, transcendentals=0),
    )(embeddings)

    near = swapped(normed, devices, 1)
    across = swapped(normed, devices, 2)
    first = shifted(normed, devices, QUAD, -2 * QUAD)
    held = {"own": normed, "near": near}
    state = products(bounds, where, held, (("own", "own"), ("near", "own")))

    later, *state = lax.optimization_barrier((normed, *state))
    second = shifted(later, devices, -2 * QUAD, QUAD)
    held["first"] = first
    state = products(bounds, where, held, (("first", "own"), ("first", "near")), state)

    across, *state = lax.optimization_barrier((across, *state))
    across_near = swapped(across, devices, 1)
    held["across"], held["second"] = across, second
    pairs = (("across", "own"), ("first", "across"), ("second", "own"), ("second", "near"), ("second", "across"))
    state = products(bounds, where, held, pairs, state)

    held = {"across_near": across_near, "own": normed, "first": first, "second": second}
    pairs = tuple((name, "across_near") for name in ("first", "second"))
    pairs = (("across_near", "own"),) + pairs
    quad, first_best, second_best = products(bounds, where, held, pairs, state, True)

    swapped_chip = swapped(quad[1::2], devices, 1)
    first_back = shifted(first_best, devices, -QUAD, 2 * QUAD)
    second_back = shifted(second_best, devices, 2 * QUAD, -QUAD)
    own_chip = jnp.maximum(quad[0::2], swapped_chip)
    swapped_quad = swapped(own_chip[1:2], devices, 2)
    best = jnp.maximum(own_chip[0:1], swapped_quad)
    even = place % 2 == 0
    from_next, from_previous = place + QUAD < devices, place >= 2 * QUAD
    filler = jnp.float32(FILLER)
    best = jnp.maximum(best, jnp.where(jnp.where(even, from_next, from_previous), first_back, filler))
    best = jnp.maximum(best, jnp.where(jnp.where(even, from_previous, from_next), second_back, filler))
    return best.reshape(length)


def solution(mesh):
    devices = 1
    for axis in AXES:
        devices *= mesh.shape[axis]
    in_specs = (P(AXES, None), P())
    return jax.shard_map(functools.partial(local, devices), mesh=mesh, in_specs=in_specs, out_specs=P(AXES), check_vma=False)
```

```python
import functools

import jax
import jax.numpy as jnp
from jax import lax
from jax.experimental import pallas as pl
from jax.experimental.pallas import tpu as pltpu
from jax.sharding import PartitionSpec as P

AXES = ("row", "col")
QUAD = 4
STRIP = 16
FILLER = -2.0
IN_QUAD = ("own", "near", "across", "across_near")
NT = (((1,), (1,)), ((), ()))


def swapped(x, devices, bit):
    return lax.ppermute(x, AXES, [(i, i ^ bit) for i in range(devices)])


def shifted(x, devices, even, odd):
    moves = [(i, i + (odd if i % 2 else even)) for i in range(devices)]
    return lax.ppermute(x, AXES, [(i, j) for i, j in moves if 0 <= j < devices])


def labels_of(bounds_ref, block, length, axis):
    shape = (length, 1) if axis == 0 else (1, length)
    positions = block * length + lax.broadcasted_iota(jnp.int32, shape, axis)
    labels = jnp.where(positions < 0, -1, 0)
    for c in range(bounds_ref.shape[0]):
        labels = labels + (bounds_ref[c] <= positions).astype(jnp.int32)
    return labels


def label_at(bounds_ref, row):
    label = jnp.where(row < 0, -1, 0)
    for c in range(bounds_ref.shape[0]):
        label = label + jnp.where(bounds_ref[c] <= row, 1, 0)
    return label


def touch(bounds_ref, one, other, length):
    lower, upper = jnp.minimum(one, other), jnp.maximum(one, other)
    return label_at(bounds_ref, (lower + 1) * length - 1) == label_at(bounds_ref, upper * length)


def masked_scores(left, right, left_labels, right_labels):
    scores = lax.dot_general(left[...], right[...], NT, preferred_element_type=jnp.float32)
    return jnp.where(left_labels == right_labels, scores, FILLER)


def folded(masked):
    result = masked[:, :128]
    for i in range(128, masked.shape[1], 128):
        result = jnp.maximum(result, masked[:, i:i + 128])
    return result


def over_rows(masked):
    return jnp.max(masked, axis=0, keepdims=True)


def normalize(raw_ref, normed_ref, scales_ref):
    for i in range(0, raw_ref.shape[0], STRIP):
        rows = pl.ds(i, STRIP)
        widened = raw_ref[rows, :].astype(jnp.float32)
        scales = lax.rsqrt(jnp.sum(widened * widened, axis=1, keepdims=True) + 1e-06)
        normed_ref[rows, :] = (widened * scales).astype(jnp.bfloat16)
        scales_ref[rows, :] = jnp.broadcast_to(scales, (STRIP, scales_ref.shape[1]))


def rescale(raw_ref, normed_ref, scales_ref, line_ref):
    scales_ref[...] = jnp.broadcast_to(line_ref[...], scales_ref.shape[::-1]).T
    for i in range(0, raw_ref.shape[0], STRIP):
        rows = pl.ds(i, STRIP)
        normed_ref[rows, :] = (raw_ref[rows, :].astype(jnp.float32) * scales_ref[rows, :1]).astype(jnp.bfloat16)


def products_kernel(names, pairs, raw, scaled, starts, ends, bounds_ref, place_ref, *refs):
    take = iter(refs)
    sources = {name: next(take) for name in names}
    lines = {name: next(take) for name in scaled}
    entering = [] if starts else [next(take) for unused in range(3)]
    quad_out, first_out, second_out = (next(take) for unused in range(3))
    normed = {name: next(take) for name in raw}
    line_out = {name: next(take) for name in raw if name not in scaled}
    scales = next(take)
    widest = dict(zip(("first", "second"), take if ends else (first_out, second_out)))
    length = sources[names[0]].shape[0]
    for i, ref in enumerate((quad_out, widest["first"], widest["second"])):
        ref[...] = jnp.full_like(ref, FILLER) if starts else entering[i][...]
    for name in raw:
        if name in scaled:
            rescale(sources[name], normed[name], scales, lines[name])
        else:
            normalize(sources[name], normed[name], scales)
            line_out[name][...] = scales[...].T[:1]
        sources[name] = normed[name]
    place = place_ref[0]
    below, above = place - QUAD, place + 2 * QUAD
    even = place % 2 == 0
    blocks = {name: place ^ b for b, name in enumerate(IN_QUAD)}
    blocks["first"], blocks["second"] = jnp.where(even, below, above), jnp.where(even, above, below)
    for left, right in pairs:

        def multiply(left=left, right=right):
            left_labels = labels_of(bounds_ref, blocks[left], length, 0)
            right_labels = labels_of(bounds_ref, blocks[right], length, 1)
            scores = masked_scores(sources[left], sources[right], left_labels, right_labels)
            if left == right:
                rows = lax.broadcasted_iota(jnp.int32, scores.shape, 0)
                columns = lax.broadcasted_iota(jnp.int32, scores.shape, 1)
                scores = jnp.where(rows == columns, FILLER, scores)
            b = IN_QUAD.index(right)
            quad_out[b:b + 1, :] = jnp.maximum(quad_out[b:b + 1, :], over_rows(scores))
            if left in widest:
                widest[left][...] = jnp.maximum(widest[left][...], folded(scores))

        if left == right:
            multiply()
        else:
            pl.when(touch(bounds_ref, blocks[left], blocks[right], length))(multiply)
    if ends:
        first_out[...] = over_rows(widest["first"][...].T)
        second_out[...] = over_rows(widest["second"][...].T)


VMEM = pl.BlockSpec(memory_space=pltpu.VMEM)
SMEM = pl.BlockSpec(memory_space=pltpu.SMEM)


def products(bounds, where, blocks, pairs, raw, scaled, state=(), ends=False):
    names = tuple(blocks)
    length, width = blocks[names[0]].shape
    folds = jax.ShapeDtypeStruct((length, 128), jnp.float32)
    line = jax.ShapeDtypeStruct((1, length), jnp.float32)
    block = jax.ShapeDtypeStruct((length, width), jnp.bfloat16)
    unscaled = [name for name in raw if name not in scaled]
    out_shape = [jax.ShapeDtypeStruct((QUAD, length), jnp.float32)] + [line if ends else folds] * 2
    out_shape += [block] * len(raw) + [line] * len(unscaled)
    results = pl.pallas_call(
        functools.partial(products_kernel, names, pairs, raw, tuple(scaled), not state, ends),
        out_shape=out_shape,
        in_specs=[SMEM, SMEM] + [VMEM] * (len(names) + len(scaled) + len(state)),
        out_specs=[VMEM] * len(out_shape),
        scratch_shapes=[pltpu.VMEM((length, 128), jnp.float32)] * (3 if ends else 1),
        compiler_params=pltpu.CompilerParams(vmem_limit_bytes=24 << 20),
        cost_estimate=pl.CostEstimate(
            flops=2 * len(pairs) * length * length * width,
            bytes_accessed=2 * len(names) * length * width,
            transcendentals=0,
        ),
    )(bounds, where, *blocks.values(), *scaled.values(), *state)
    normed = dict(zip(raw, results[3:]))
    return results[:3], {**blocks, **normed}, results[3 + len(raw):]


def local(devices, embeddings, cluster_sizes):
    length = embeddings.shape[0]
    place = lax.axis_index(AXES).astype(jnp.int32)
    bounds = jnp.cumsum(cluster_sizes).astype(jnp.int32)
    where = place.reshape(1)

    near = swapped(embeddings, devices, 1)
    across = swapped(embeddings, devices, 2)
    first = shifted(embeddings, devices, QUAD, -2 * QUAD)
    held = {"own": embeddings, "near": near}
    pairs = (("own", "own"), ("near", "own"))
    state, held, (own_scales, near_scales) = products(bounds, where, held, pairs, ("own", "near"), {})

    later, own_scales = lax.optimization_barrier((embeddings, own_scales))
    second = shifted(later, devices, -2 * QUAD, QUAD)
    second_scales = shifted(own_scales, devices, -2 * QUAD, QUAD)
    across_scales = swapped(jnp.concatenate([own_scales, near_scales]), devices, 2)
    first, second_scales, across_scales = lax.optimization_barrier((first, second_scales, across_scales))

    pairs = (("first", "own"), ("first", "near"))
    state, held, unused = products(bounds, where, {**held, "first": first}, pairs, ("first",), {}, state)

    across, *state = lax.optimization_barrier((across, *state))
    across_near = swapped(across, devices, 1)
    held["across"], held["second"] = across, second
    pairs = (("across", "own"), ("first", "across"), ("second", "own"), ("second", "near"), ("second", "across"))
    scales = {"across": across_scales[:1], "second": second_scales}
    state, held, unused = products(bounds, where, held, pairs, ("across", "second"), scales, state)

    held = {name: held[name] for name in ("own", "first", "second")}
    held["across_near"] = across_near
    pairs = (("across_near", "own"), ("first", "across_near"), ("second", "across_near"))
    scales = {"across_near": across_scales[1:]}
    state, unused, unused = products(bounds, where, held, pairs, ("across_near",), scales, state, True)
    quad, first_best, second_best = state

    swapped_chip = swapped(quad[1::2], devices, 1)
    first_back = shifted(first_best, devices, -QUAD, 2 * QUAD)
    second_back = shifted(second_best, devices, 2 * QUAD, -QUAD)
    own_chip = jnp.maximum(quad[0::2], swapped_chip)
    swapped_quad = swapped(own_chip[1:2], devices, 2)
    best = jnp.maximum(own_chip[0:1], swapped_quad)
    even = place % 2 == 0
    from_next, from_previous = place + QUAD < devices, place >= 2 * QUAD
    filler = jnp.float32(FILLER)
    best = jnp.maximum(best, jnp.where(jnp.where(even, from_next, from_previous), first_back, filler))
    best = jnp.maximum(best, jnp.where(jnp.where(even, from_previous, from_next), second_back, filler))
    return best.reshape(length)


def solution(mesh):
    devices = 1
    for axis in AXES:
        devices *= mesh.shape[axis]
    in_specs = (P(AXES, None), P())
    return jax.shard_map(functools.partial(local, devices), mesh=mesh, in_specs=in_specs, out_specs=P(AXES), check_vma=False)
```

```python
import functools

import jax
import jax.numpy as jnp
from jax import lax
from jax.experimental import pallas as pl
from jax.experimental.pallas import tpu as pltpu
from jax.sharding import PartitionSpec as P

AXES = ("row", "col")
QUAD = 4
STRIP = 16
FILLER = -2.0
IN_QUAD = ("own", "near", "across", "across_near")
NT = (((1,), (1,)), ((), ()))


def swapped(x, devices, bit):
    return lax.ppermute(x, AXES, [(i, i ^ bit) for i in range(devices)])


def shifted(x, devices, even, odd):
    moves = [(i, i + (odd if i % 2 else even)) for i in range(devices)]
    return lax.ppermute(x, AXES, [(i, j) for i, j in moves if 0 <= j < devices])


def labels_of(bounds_ref, block, length, axis):
    shape = (length, 1) if axis == 0 else (1, length)
    positions = block * length + lax.broadcasted_iota(jnp.int32, shape, axis)
    labels = jnp.where(positions < 0, -1, 0)
    for c in range(bounds_ref.shape[0]):
        labels = labels + (bounds_ref[c] <= positions).astype(jnp.int32)
    return labels


def label_at(bounds_ref, row):
    label = jnp.where(row < 0, -1, 0)
    for c in range(bounds_ref.shape[0]):
        label = label + jnp.where(bounds_ref[c] <= row, 1, 0)
    return label


def touch(bounds_ref, one, other, length):
    lower, upper = jnp.minimum(one, other), jnp.maximum(one, other)
    return label_at(bounds_ref, (lower + 1) * length - 1) == label_at(bounds_ref, upper * length)


def masked_scores(left, right, left_labels, right_labels):
    scores = lax.dot_general(left[...], right[...], NT, preferred_element_type=jnp.float32)
    return jnp.where(left_labels == right_labels, scores, FILLER)


def folded(masked):
    result = masked[:, :128]
    for i in range(128, masked.shape[1], 128):
        result = jnp.maximum(result, masked[:, i:i + 128])
    return result


def over_rows(masked):
    return jnp.max(masked, axis=0, keepdims=True)


def normalize_kernel(raw_hbm, normed, raw, sems):
    pieces = sems.shape[0]
    length = raw.shape[0] // pieces
    copies = []
    for i in range(pieces):
        rows = pl.ds(i * length, length)
        copies.append(pltpu.make_async_copy(raw_hbm.at[rows], raw.at[rows], sems.at[i]))
    for copy in copies:
        copy.start()
    for i in range(pieces):
        copies[i].wait()
        for j in range(0, length, STRIP):
            rows = pl.ds(i * length + j, STRIP)
            widened = raw[rows, :].astype(jnp.float32)
            squares = jnp.sum(widened * widened, axis=1, keepdims=True) + 1e-06
            normed[rows, :] = (widened * lax.rsqrt(squares)).astype(jnp.bfloat16)


def products_kernel(names, pairs, starts, ends, bounds_ref, place_ref, *refs):
    sources, refs = refs[:len(names)], refs[len(names):]
    if not starts:
        entering, refs = refs[:3], refs[3:]
    quad_out, first_out, second_out = refs[:3]
    widest = dict(zip(("first", "second"), refs[3:] if ends else (first_out, second_out)))
    length = sources[0].shape[0]
    for i, ref in enumerate((quad_out, widest["first"], widest["second"])):
        ref[...] = jnp.full_like(ref, FILLER) if starts else entering[i][...]
    place = place_ref[0]
    below, above = place - QUAD, place + 2 * QUAD
    even = place % 2 == 0
    blocks = {name: place ^ b for b, name in enumerate(IN_QUAD)}
    blocks["first"], blocks["second"] = jnp.where(even, below, above), jnp.where(even, above, below)
    left_labels = {name: labels_of(bounds_ref, blocks[name], length, 0) for name in {pair[0]: 0 for pair in pairs}}
    right_labels = {name: labels_of(bounds_ref, blocks[name], length, 1) for name in {pair[1]: 0 for pair in pairs}}
    for left, right in pairs:

        def multiply(left=left, right=right):
            pair = sources[names.index(left)], sources[names.index(right)]
            scores = masked_scores(*pair, left_labels[left], right_labels[right])
            if left == right:
                rows = lax.broadcasted_iota(jnp.int32, scores.shape, 0)
                columns = lax.broadcasted_iota(jnp.int32, scores.shape, 1)
                scores = jnp.where(rows == columns, FILLER, scores)
            b = IN_QUAD.index(right)
            quad_out[b:b + 1, :] = jnp.maximum(quad_out[b:b + 1, :], over_rows(scores))
            if left in widest:
                widest[left][...] = jnp.maximum(widest[left][...], folded(scores))

        if left == right:
            multiply()
        else:
            pl.when(touch(bounds_ref, blocks[left], blocks[right], length))(multiply)
    if ends:
        first_out[...] = over_rows(widest["first"][...].T)
        second_out[...] = over_rows(widest["second"][...].T)


HBM = pl.BlockSpec(memory_space=pltpu.HBM)
VMEM = pl.BlockSpec(memory_space=pltpu.VMEM)
SMEM = pl.BlockSpec(memory_space=pltpu.SMEM)


def products(bounds, where, blocks, pairs, state=None, ends=False):
    names = tuple(blocks)
    length, width = blocks[names[0]].shape
    folds = jax.ShapeDtypeStruct((length, 128), jnp.float32)
    line = jax.ShapeDtypeStruct((1, length), jnp.float32)
    entering = () if state is None else state
    return pl.pallas_call(
        functools.partial(products_kernel, names, pairs, state is None, ends),
        out_shape=(jax.ShapeDtypeStruct((QUAD, length), jnp.float32),) + ((line, line) if ends else (folds, folds)),
        in_specs=[SMEM, SMEM] + [VMEM] * (len(names) + len(entering)),
        out_specs=(VMEM,) * 3,
        scratch_shapes=[pltpu.VMEM((length, 128), jnp.float32)] * (2 if ends else 0),
        compiler_params=pltpu.CompilerParams(vmem_limit_bytes=24 << 20),
        cost_estimate=pl.CostEstimate(
            flops=2 * len(pairs) * length * length * width,
            bytes_accessed=2 * len(names) * length * width,
            transcendentals=0,
        ),
    )(bounds, where, *blocks.values(), *entering)


def local(devices, embeddings, cluster_sizes):
    length, width = embeddings.shape
    place = lax.axis_index(AXES).astype(jnp.int32)
    bounds = jnp.cumsum(cluster_sizes).astype(jnp.int32)
    where = place.reshape(1)

    normed = pl.pallas_call(
        normalize_kernel,
        out_shape=jax.ShapeDtypeStruct((length, width), jnp.bfloat16),
        in_specs=[HBM],
        out_specs=VMEM,
        scratch_shapes=[pltpu.VMEM((length, width), jnp.bfloat16), pltpu.SemaphoreType.DMA((4,))],
        compiler_params=pltpu.CompilerParams(vmem_limit_bytes=50 << 20),
        cost_estimate=pl.CostEstimate(flops=0, bytes_accessed=4 * length * width, transcendentals=0),
    )(embeddings)

    near = swapped(normed, devices, 1)
    across = swapped(normed, devices, 2)
    first = shifted(normed, devices, QUAD, -2 * QUAD)
    held = {"own": normed, "near": near}
    state = products(bounds, where, held, (("own", "own"), ("near", "own")))

    later, *state = lax.optimization_barrier((normed, *state))
    second = shifted(later, devices, -2 * QUAD, QUAD)
    held["first"] = first
    state = products(bounds, where, held, (("first", "own"), ("first", "near")), state)

    across, *state = lax.optimization_barrier((across, *state))
    across_near = swapped(across, devices, 1)
    held["across"], held["second"] = across, second
    pairs = (("across", "own"), ("first", "across"), ("second", "own"), ("second", "near"), ("second", "across"))
    state = products(bounds, where, held, pairs, state)

    held = {"across_near": across_near, "own": normed, "first": first, "second": second}
    pairs = tuple((name, "across_near") for name in ("first", "second"))
    pairs = (("across_near", "own"),) + pairs
    quad, first_best, second_best = products(bounds, where, held, pairs, state, True)

    swapped_chip = swapped(quad[1::2], devices, 1)
    first_back = shifted(first_best, devices, -QUAD, 2 * QUAD)
    second_back = shifted(second_best, devices, 2 * QUAD, -QUAD)
    own_chip = jnp.maximum(quad[0::2], swapped_chip)
    swapped_quad = swapped(own_chip[1:2], devices, 2)
    best = jnp.maximum(own_chip[0:1], swapped_quad)
    even = place % 2 == 0
    from_next, from_previous = place + QUAD < devices, place >= 2 * QUAD
    filler = jnp.float32(FILLER)
    best = jnp.maximum(best, jnp.where(jnp.where(even, from_next, from_previous), first_back, filler))
    best = jnp.maximum(best, jnp.where(jnp.where(even, from_previous, from_next), second_back, filler))
    return best.reshape(length)


def solution(mesh):
    devices = 1
    for axis in AXES:
        devices *= mesh.shape[axis]
    in_specs = (P(AXES, None), P())
    return jax.shard_map(functools.partial(local, devices), mesh=mesh, in_specs=in_specs, out_specs=P(AXES), check_vma=False)
```

```python
import functools

import jax
import jax.numpy as jnp
from jax import lax
from jax.experimental import pallas as pl
from jax.experimental.pallas import tpu as pltpu
from jax.sharding import PartitionSpec as P

AXES = ("row", "col")
QUAD = 4
STRIP = 16
FILLER = -2.0
IN_QUAD = ("own", "near", "across", "across_near")
NT = (((1,), (1,)), ((), ()))


def swapped(x, devices, bit):
    return lax.ppermute(x, AXES, [(i, i ^ bit) for i in range(devices)])


def shifted(x, devices, even, odd):
    moves = [(i, i + (odd if i % 2 else even)) for i in range(devices)]
    return lax.ppermute(x, AXES, [(i, j) for i, j in moves if 0 <= j < devices])


def labels_of(bounds_ref, block, length, axis):
    shape = (length, 1) if axis == 0 else (1, length)
    positions = block * length + lax.broadcasted_iota(jnp.int32, shape, axis)
    labels = jnp.where(positions < 0, -1, 0)
    for c in range(bounds_ref.shape[0]):
        labels = labels + (bounds_ref[c] <= positions).astype(jnp.int32)
    return labels


def label_at(bounds_ref, row):
    label = jnp.where(row < 0, -1, 0)
    for c in range(bounds_ref.shape[0]):
        label = label + jnp.where(bounds_ref[c] <= row, 1, 0)
    return label


def touch(bounds_ref, one, other, length):
    lower, upper = jnp.minimum(one, other), jnp.maximum(one, other)
    return label_at(bounds_ref, (lower + 1) * length - 1) == label_at(bounds_ref, upper * length)


def masked_scores(left, right, left_labels, right_labels):
    scores = lax.dot_general(left[...], right[...], NT, preferred_element_type=jnp.float32)
    return jnp.where(left_labels == right_labels, scores, FILLER)


def folded(masked):
    result = masked[:, :128]
    for i in range(128, masked.shape[1], 128):
        result = jnp.maximum(result, masked[:, i:i + 128])
    return result


def over_rows(masked):
    return jnp.max(masked, axis=0, keepdims=True)


def normalize_kernel(raw_hbm, normed, raw, sems):
    pieces = sems.shape[0]
    length = raw.shape[0] // pieces
    copies = []
    for i in range(pieces):
        rows = pl.ds(i * length, length)
        copies.append(pltpu.make_async_copy(raw_hbm.at[rows], raw.at[rows], sems.at[i]))
    for copy in copies:
        copy.start()
    for i in range(pieces):
        copies[i].wait()
        for j in range(0, length, STRIP):
            rows = pl.ds(i * length + j, STRIP)
            widened = raw[rows, :].astype(jnp.float32)
            squares = jnp.sum(widened * widened, axis=1, keepdims=True) + 1e-06
            normed[rows, :] = (widened * lax.rsqrt(squares)).astype(jnp.bfloat16)


def products_kernel(names, pairs, keep, starts, ends, bounds_ref, place_ref, *refs):
    sources, refs = refs[:len(names)], refs[len(names):]
    if not starts:
        entering, refs = refs[:3], refs[3:]
    (quad_out, first_out, second_out), kept, refs = refs[:3], refs[3:3 + len(keep)], refs[3 + len(keep):]
    widest = dict(zip(("first", "second"), refs if ends else (first_out, second_out)))
    length = sources[0].shape[0]
    for i, ref in enumerate((quad_out, widest["first"], widest["second"])):
        ref[...] = jnp.full_like(ref, FILLER) if starts else entering[i][...]
    place = place_ref[0]
    below, above = place - QUAD, place + 2 * QUAD
    even = place % 2 == 0
    blocks = {name: place ^ b for b, name in enumerate(IN_QUAD)}
    blocks["first"], blocks["second"] = jnp.where(even, below, above), jnp.where(even, above, below)
    left_labels = {name: labels_of(bounds_ref, blocks[name], length, 0) for name in {pair[0]: 0 for pair in pairs}}
    right_labels = {name: labels_of(bounds_ref, blocks[name], length, 1) for name in {pair[1]: 0 for pair in pairs}}
    for left, right in pairs:

        def multiply(left=left, right=right):
            pair = sources[names.index(left)], sources[names.index(right)]
            scores = masked_scores(*pair, left_labels[left], right_labels[right])
            if left == right:
                rows = lax.broadcasted_iota(jnp.int32, scores.shape, 0)
                columns = lax.broadcasted_iota(jnp.int32, scores.shape, 1)
                scores = jnp.where(rows == columns, FILLER, scores)
            b = IN_QUAD.index(right)
            quad_out[b:b + 1, :] = jnp.maximum(quad_out[b:b + 1, :], over_rows(scores))
            if left in widest:
                widest[left][...] = jnp.maximum(widest[left][...], folded(scores))

        if left == right:
            multiply()
        else:
            pl.when(touch(bounds_ref, blocks[left], blocks[right], length))(multiply)
    for name, ref in zip(keep, kept):
        ref[...] = sources[names.index(name)][...]
    if ends:
        first_out[...] = over_rows(widest["first"][...].T)
        second_out[...] = over_rows(widest["second"][...].T)


HBM = pl.BlockSpec(memory_space=pltpu.HBM)
VMEM = pl.BlockSpec(memory_space=pltpu.VMEM)
SMEM = pl.BlockSpec(memory_space=pltpu.SMEM)


def products(bounds, where, blocks, pairs, state=None, ends=False, keep=()):
    names = tuple(blocks)
    length, width = blocks[names[0]].shape
    folds = jax.ShapeDtypeStruct((length, 128), jnp.float32)
    line = jax.ShapeDtypeStruct((1, length), jnp.float32)
    block = jax.ShapeDtypeStruct((length, width), jnp.bfloat16)
    entering = () if state is None else state
    results = pl.pallas_call(
        functools.partial(products_kernel, names, pairs, keep, state is None, ends),
        out_shape=(jax.ShapeDtypeStruct((QUAD, length), jnp.float32),) + ((line, line) if ends else (folds, folds)) + (block,) * len(keep),
        in_specs=[SMEM, SMEM] + [VMEM] * (len(names) + len(entering)),
        out_specs=(VMEM,) * (3 + len(keep)),
        scratch_shapes=[pltpu.VMEM((length, 128), jnp.float32)] * (2 if ends else 0),
        compiler_params=pltpu.CompilerParams(vmem_limit_bytes=24 << 20),
        cost_estimate=pl.CostEstimate(
            flops=0,
            bytes_accessed=0,
            transcendentals=0,
        ),
    )(bounds, where, *blocks.values(), *entering)
    return results[:3], {**blocks, **dict(zip(keep, results[3:]))}


def local(devices, embeddings, cluster_sizes):
    length, width = embeddings.shape
    place = lax.axis_index(AXES).astype(jnp.int32)
    bounds = jnp.cumsum(cluster_sizes).astype(jnp.int32)
    where = place.reshape(1)

    normed = pl.pallas_call(
        normalize_kernel,
        out_shape=jax.ShapeDtypeStruct((length, width), jnp.bfloat16),
        in_specs=[HBM],
        out_specs=VMEM,
        scratch_shapes=[pltpu.VMEM((length, width), jnp.bfloat16), pltpu.SemaphoreType.DMA((4,))],
        compiler_params=pltpu.CompilerParams(vmem_limit_bytes=50 << 20),
        cost_estimate=pl.CostEstimate(flops=0, bytes_accessed=4 * length * width, transcendentals=0),
    )(embeddings)

    near = swapped(normed, devices, 1)
    across = swapped(normed, devices, 2)
    first = shifted(normed, devices, QUAD, -2 * QUAD)
    pairs = (("own", "own"), ("near", "own"))
    state, held = products(bounds, where, {"own": normed, "near": near}, pairs, keep=("near",))

    later, *state = lax.optimization_barrier((normed, *state))
    second = shifted(later, devices, -2 * QUAD, QUAD)

    across, *state = lax.optimization_barrier((across, *state))
    across_near = swapped(across, devices, 1)
    held["across"], held["first"] = across, first
    pairs = (("across", "own"), ("first", "own"), ("first", "near"), ("first", "across"))
    state, held = products(bounds, where, held, pairs, state, keep=("across", "first"))

    held["second"] = second
    pairs = (("second", "own"), ("second", "near"), ("second", "across"))
    state, held = products(bounds, where, held, pairs, state)

    held["across_near"] = across_near
    del held["near"], held["across"]
    pairs = (("across_near", "own"), ("first", "across_near"), ("second", "across_near"))
    (quad, first_best, second_best), unused = products(bounds, where, held, pairs, state, ends=True)

    swapped_chip = swapped(quad[1::2], devices, 1)
    first_back = shifted(first_best, devices, -QUAD, 2 * QUAD)
    second_back = shifted(second_best, devices, 2 * QUAD, -QUAD)
    own_chip = jnp.maximum(quad[0::2], swapped_chip)
    swapped_quad = swapped(own_chip[1:2], devices, 2)
    best = jnp.maximum(own_chip[0:1], swapped_quad)
    even = place % 2 == 0
    from_next, from_previous = place + QUAD < devices, place >= 2 * QUAD
    filler = jnp.float32(FILLER)
    best = jnp.maximum(best, jnp.where(jnp.where(even, from_next, from_previous), first_back, filler))
    best = jnp.maximum(best, jnp.where(jnp.where(even, from_previous, from_next), second_back, filler))
    return best.reshape(length)


def solution(mesh):
    devices = 1
    for axis in AXES:
        devices *= mesh.shape[axis]
    in_specs = (P(AXES, None), P())
    return jax.shard_map(functools.partial(local, devices), mesh=mesh, in_specs=in_specs, out_specs=P(AXES), check_vma=False)
```

```python
import functools

import jax
import jax.numpy as jnp
from jax import lax
from jax.experimental import pallas as pl
from jax.experimental.pallas import tpu as pltpu
from jax.sharding import PartitionSpec as P

AXES = ("row", "col")
QUAD = 4
STRIP = 16
FILLER = -2.0
IN_QUAD = ("own", "near", "across", "across_near")
NT = (((1,), (1,)), ((), ()))


def swapped(x, devices, bit):
    return lax.ppermute(x, AXES, [(i, i ^ bit) for i in range(devices)])


def shifted(x, devices, even, odd):
    moves = [(i, i + (odd if i % 2 else even)) for i in range(devices)]
    return lax.ppermute(x, AXES, [(i, j) for i, j in moves if 0 <= j < devices])


def labels_of(bounds_ref, block, length, axis):
    shape = (length, 1) if axis == 0 else (1, length)
    positions = block * length + lax.broadcasted_iota(jnp.int32, shape, axis)
    labels = jnp.where(positions < 0, -1, 0)
    for c in range(bounds_ref.shape[0]):
        labels = labels + (bounds_ref[c] <= positions).astype(jnp.int32)
    return labels


def label_at(bounds_ref, row):
    label = jnp.where(row < 0, -1, 0)
    for c in range(bounds_ref.shape[0]):
        label = label + jnp.where(bounds_ref[c] <= row, 1, 0)
    return label


def touch(bounds_ref, one, other, length):
    lower, upper = jnp.minimum(one, other), jnp.maximum(one, other)
    return label_at(bounds_ref, (lower + 1) * length - 1) == label_at(bounds_ref, upper * length)


def masked_scores(left, right, left_labels, right_labels):
    scores = lax.dot_general(left[...], right[...], NT, preferred_element_type=jnp.float32)
    return jnp.where(left_labels == right_labels, scores, FILLER)


def folded(masked):
    result = masked[:, :128]
    for i in range(128, masked.shape[1], 128):
        result = jnp.maximum(result, masked[:, i:i + 128])
    return result


def over_rows(masked):
    return jnp.max(masked, axis=0, keepdims=True)


def normalize_kernel(raw_hbm, normed, raw, sems):
    pieces = sems.shape[0]
    length = raw.shape[0] // pieces
    copies = []
    for i in range(pieces):
        rows = pl.ds(i * length, length)
        copies.append(pltpu.make_async_copy(raw_hbm.at[rows], raw.at[rows], sems.at[i]))
    for copy in copies:
        copy.start()
    for i in range(pieces):
        copies[i].wait()
        for j in range(0, length, STRIP):
            rows = pl.ds(i * length + j, STRIP)
            widened = raw[rows, :].astype(jnp.float32)
            squares = jnp.sum(widened * widened, axis=1, keepdims=True) + 1e-06
            normed[rows, :] = (widened * lax.rsqrt(squares)).astype(jnp.bfloat16)


def products_kernel(names, pairs, keep, starts, ends, bounds_ref, place_ref, *refs):
    sources, refs = refs[:len(names)], refs[len(names):]
    if not starts:
        entering, refs = refs[:3], refs[3:]
    (quad_out, first_out, second_out), kept, refs = refs[:3], refs[3:3 + len(keep)], refs[3 + len(keep):]
    widest = dict(zip(("first", "second"), refs if ends else (first_out, second_out)))
    length = sources[0].shape[0]
    for i, ref in enumerate((quad_out, widest["first"], widest["second"])):
        ref[...] = jnp.full_like(ref, FILLER) if starts else entering[i][...]
    place = place_ref[0]
    below, above = place - QUAD, place + 2 * QUAD
    even = place % 2 == 0
    blocks = {name: place ^ b for b, name in enumerate(IN_QUAD)}
    blocks["first"], blocks["second"] = jnp.where(even, below, above), jnp.where(even, above, below)
    left_labels = {name: labels_of(bounds_ref, blocks[name], length, 0) for name in {pair[0]: 0 for pair in pairs}}
    right_labels = {name: labels_of(bounds_ref, blocks[name], length, 1) for name in {pair[1]: 0 for pair in pairs}}
    for left, right in pairs:

        def multiply(left=left, right=right):
            pair = sources[names.index(left)], sources[names.index(right)]
            scores = masked_scores(*pair, left_labels[left], right_labels[right])
            if left == right:
                rows = lax.broadcasted_iota(jnp.int32, scores.shape, 0)
                columns = lax.broadcasted_iota(jnp.int32, scores.shape, 1)
                scores = jnp.where(rows == columns, FILLER, scores)
            b = IN_QUAD.index(right)
            quad_out[b:b + 1, :] = jnp.maximum(quad_out[b:b + 1, :], over_rows(scores))
            if left in widest:
                widest[left][...] = jnp.maximum(widest[left][...], folded(scores))

        if left == right:
            multiply()
        else:
            pl.when(touch(bounds_ref, blocks[left], blocks[right], length))(multiply)
    for name, ref in zip(keep, kept):
        ref[...] = sources[names.index(name)][...]
    if ends:
        first_out[...] = over_rows(widest["first"][...].T)
        second_out[...] = over_rows(widest["second"][...].T)


HBM = pl.BlockSpec(memory_space=pltpu.HBM)
VMEM = pl.BlockSpec(memory_space=pltpu.VMEM)
SMEM = pl.BlockSpec(memory_space=pltpu.SMEM)


def products(bounds, where, blocks, pairs, state=None, ends=False, keep=()):
    names = tuple(blocks)
    length, width = blocks[names[0]].shape
    folds = jax.ShapeDtypeStruct((length, 128), jnp.float32)
    line = jax.ShapeDtypeStruct((1, length), jnp.float32)
    block = jax.ShapeDtypeStruct((length, width), jnp.bfloat16)
    entering = () if state is None else state
    results = pl.pallas_call(
        functools.partial(products_kernel, names, pairs, keep, state is None, ends),
        out_shape=(jax.ShapeDtypeStruct((QUAD, length), jnp.float32),) + ((line, line) if ends else (folds, folds)) + (block,) * len(keep),
        in_specs=[SMEM, SMEM] + [VMEM] * (len(names) + len(entering)),
        out_specs=(VMEM,) * (3 + len(keep)),
        scratch_shapes=[pltpu.VMEM((length, 128), jnp.float32)] * (2 if ends else 0),
        compiler_params=pltpu.CompilerParams(vmem_limit_bytes=24 << 20),
        cost_estimate=pl.CostEstimate(
            flops=0,
            bytes_accessed=0,
            transcendentals=0,
        ),
    )(bounds, where, *blocks.values(), *entering)
    return results[:3], {**blocks, **dict(zip(keep, results[3:]))}


def local(devices, embeddings, cluster_sizes):
    length, width = embeddings.shape
    place = lax.axis_index(AXES).astype(jnp.int32)
    bounds = jnp.cumsum(cluster_sizes).astype(jnp.int32)
    where = place.reshape(1)

    normed = pl.pallas_call(
        normalize_kernel,
        out_shape=jax.ShapeDtypeStruct((length, width), jnp.bfloat16),
        in_specs=[HBM],
        out_specs=VMEM,
        scratch_shapes=[pltpu.VMEM((length, width), jnp.bfloat16), pltpu.SemaphoreType.DMA((4,))],
        compiler_params=pltpu.CompilerParams(vmem_limit_bytes=50 << 20),
        cost_estimate=pl.CostEstimate(flops=0, bytes_accessed=4 * length * width, transcendentals=0),
    )(embeddings)

    near = swapped(normed, devices, 1)
    across = swapped(normed, devices, 2)
    first = shifted(normed, devices, QUAD, -2 * QUAD)
    pairs = (("own", "own"), ("near", "own"))
    state, held = products(bounds, where, {"own": normed, "near": near}, pairs, keep=("near",))

    later, *state = lax.optimization_barrier((normed, *state))
    second = shifted(later, devices, -2 * QUAD, QUAD)

    across, *state = lax.optimization_barrier((across, *state))
    across_near = swapped(across, devices, 1)
    held["across"], held["first"] = across, first
    pairs = (("across", "own"), ("first", "own"), ("first", "near"), ("first", "across"))
    state, held = products(bounds, where, held, pairs, state, keep=("across", "first"))

    held["second"] = second
    pairs = (("second", "own"), ("second", "near"), ("second", "across"))
    state, held = products(bounds, where, held, pairs, state)

    held["across_near"] = across_near
    del held["near"], held["across"]
    pairs = (("across_near", "own"), ("first", "across_near"), ("second", "across_near"))
    (quad, first_best, second_best), unused = products(bounds, where, held, pairs, state, ends=True)

    received = swapped(jnp.concatenate([quad[1::2], second_best]), devices, 1)
    own_chip = jnp.maximum(quad[0::2], received[:2])
    outside = shifted(jnp.concatenate([first_best, received[2:]]), devices, -QUAD, 2 * QUAD)
    swapped_quad = swapped(own_chip[1:], devices, 2)
    even = place % 2 == 0
    landed = jnp.where(even, place + QUAD < devices, place >= 2 * QUAD)
    outside = jnp.where(landed, outside, jnp.float32(FILLER))
    swapped_outside = swapped(outside[1:], devices, 1)
    best = jnp.maximum(jnp.maximum(own_chip[:1], swapped_quad), jnp.maximum(outside[:1], swapped_outside))
    return best.reshape(length)


def solution(mesh):
    devices = 1
    for axis in AXES:
        devices *= mesh.shape[axis]
    in_specs = (P(AXES, None), P())
    return jax.shard_map(functools.partial(local, devices), mesh=mesh, in_specs=in_specs, out_specs=P(AXES), check_vma=False)
```

```python
import functools

import jax
import jax.numpy as jnp
from jax import lax
from jax.experimental import pallas as pl
from jax.experimental.pallas import tpu as pltpu
from jax.sharding import PartitionSpec as P

AXES = ("row", "col")
QUAD = 4
STRIP = 16
FILLER = -2.0
IN_QUAD = ("own", "near", "across", "across_near")
NT = (((1,), (1,)), ((), ()))


def swapped(x, devices, bit):
    return lax.ppermute(x, AXES, [(i, i ^ bit) for i in range(devices)])


def shifted(x, devices, even, odd):
    moves = [(i, i + (odd if i % 2 else even)) for i in range(devices)]
    return lax.ppermute(x, AXES, [(i, j) for i, j in moves if 0 <= j < devices])


def spans_of(bounds_ref, block, length):
    positions = block * length + lax.broadcasted_iota(jnp.int32, (1, length), 1)
    starts, ends = jnp.zeros_like(positions), jnp.full_like(positions, jnp.iinfo(jnp.int32).max)
    for c in range(bounds_ref.shape[0]):
        bound = bounds_ref[c]
        passed = bound <= positions
        starts = jnp.where(passed, jnp.maximum(starts, bound), starts)
        ends = jnp.where(passed, ends, jnp.minimum(ends, bound))
    return starts, ends


def label_at(bounds_ref, row):
    label = jnp.where(row < 0, -1, 0)
    for c in range(bounds_ref.shape[0]):
        label = label + jnp.where(bounds_ref[c] <= row, 1, 0)
    return label


def touch(bounds_ref, one, other, length):
    lower, upper = jnp.minimum(one, other), jnp.maximum(one, other)
    return label_at(bounds_ref, (lower + 1) * length - 1) == label_at(bounds_ref, upper * length)


def masked_scores(left, right, block, spans):
    scores = lax.dot_general(left[...], right[...], NT, preferred_element_type=jnp.float32)
    positions = block * left.shape[0] + lax.broadcasted_iota(jnp.int32, scores.shape, 0)
    return jnp.where((positions >= spans[0]) & (positions < spans[1]), scores, FILLER)


def folded(masked):
    result = masked[:, :128]
    for i in range(128, masked.shape[1], 128):
        result = jnp.maximum(result, masked[:, i:i + 128])
    return result


def over_rows(masked):
    return jnp.max(masked, axis=0, keepdims=True)


def normalize_kernel(raw_hbm, normed, raw, sems):
    pieces = sems.shape[0]
    length = raw.shape[0] // pieces
    copies = []
    for i in range(pieces):
        rows = pl.ds(i * length, length)
        copies.append(pltpu.make_async_copy(raw_hbm.at[rows], raw.at[rows], sems.at[i]))
    for copy in copies:
        copy.start()
    for i in range(pieces):
        copies[i].wait()
        for j in range(0, length, STRIP):
            rows = pl.ds(i * length + j, STRIP)
            widened = raw[rows, :].astype(jnp.float32)
            squares = jnp.sum(widened * widened, axis=1, keepdims=True) + 1e-06
            normed[rows, :] = (widened * lax.rsqrt(squares)).astype(jnp.bfloat16)


def products_kernel(names, pairs, keep, starts, ends, bounds_ref, place_ref, *refs):
    sources, refs = refs[:len(names)], refs[len(names):]
    if not starts:
        entering, refs = refs[:3], refs[3:]
    (quad_out, first_out, second_out), kept, refs = refs[:3], refs[3:3 + len(keep)], refs[3 + len(keep):]
    widest = dict(zip(("first", "second"), refs if ends else (first_out, second_out)))
    length = sources[0].shape[0]
    for i, ref in enumerate((quad_out, widest["first"], widest["second"])):
        ref[...] = jnp.full_like(ref, FILLER) if starts else entering[i][...]
    place = place_ref[0]
    below, above = place - QUAD, place + 2 * QUAD
    even = place % 2 == 0
    blocks = {name: place ^ b for b, name in enumerate(IN_QUAD)}
    blocks["first"], blocks["second"] = jnp.where(even, below, above), jnp.where(even, above, below)
    spans = {name: spans_of(bounds_ref, blocks[name], length) for name in {pair[1]: 0 for pair in pairs}}
    for left, right in pairs:

        def multiply(left=left, right=right):
            pair = sources[names.index(left)], sources[names.index(right)]
            scores = masked_scores(*pair, blocks[left], spans[right])
            if left == right:
                rows = lax.broadcasted_iota(jnp.int32, scores.shape, 0)
                columns = lax.broadcasted_iota(jnp.int32, scores.shape, 1)
                scores = jnp.where(rows == columns, FILLER, scores)
            b = IN_QUAD.index(right)
            quad_out[b:b + 1, :] = jnp.maximum(quad_out[b:b + 1, :], over_rows(scores))
            if left in widest:
                widest[left][...] = jnp.maximum(widest[left][...], folded(scores))

        if left == right:
            multiply()
        else:
            pl.when(touch(bounds_ref, blocks[left], blocks[right], length))(multiply)
    for name, ref in zip(keep, kept):
        ref[...] = sources[names.index(name)][...]
    if ends:
        first_out[...] = over_rows(widest["first"][...].T)
        second_out[...] = over_rows(widest["second"][...].T)


HBM = pl.BlockSpec(memory_space=pltpu.HBM)
VMEM = pl.BlockSpec(memory_space=pltpu.VMEM)
SMEM = pl.BlockSpec(memory_space=pltpu.SMEM)


def products(bounds, where, blocks, pairs, state=None, ends=False, keep=()):
    names = tuple(blocks)
    length, width = blocks[names[0]].shape
    folds = jax.ShapeDtypeStruct((length, 128), jnp.float32)
    line = jax.ShapeDtypeStruct((1, length), jnp.float32)
    block = jax.ShapeDtypeStruct((length, width), jnp.bfloat16)
    entering = () if state is None else state
    results = pl.pallas_call(
        functools.partial(products_kernel, names, pairs, keep, state is None, ends),
        out_shape=(jax.ShapeDtypeStruct((QUAD, length), jnp.float32),) + ((line, line) if ends else (folds, folds)) + (block,) * len(keep),
        in_specs=[SMEM, SMEM] + [VMEM] * (len(names) + len(entering)),
        out_specs=(VMEM,) * (3 + len(keep)),
        scratch_shapes=[pltpu.VMEM((length, 128), jnp.float32)] * (2 if ends else 0),
        compiler_params=pltpu.CompilerParams(vmem_limit_bytes=24 << 20),
        cost_estimate=pl.CostEstimate(
            flops=0,
            bytes_accessed=0,
            transcendentals=0,
        ),
    )(bounds, where, *blocks.values(), *entering)
    return results[:3], {**blocks, **dict(zip(keep, results[3:]))}


def local(devices, embeddings, cluster_sizes):
    length, width = embeddings.shape
    place = lax.axis_index(AXES).astype(jnp.int32)
    bounds = jnp.cumsum(cluster_sizes).astype(jnp.int32)
    where = place.reshape(1)

    normed = pl.pallas_call(
        normalize_kernel,
        out_shape=jax.ShapeDtypeStruct((length, width), jnp.bfloat16),
        in_specs=[HBM],
        out_specs=VMEM,
        scratch_shapes=[pltpu.VMEM((length, width), jnp.bfloat16), pltpu.SemaphoreType.DMA((4,))],
        compiler_params=pltpu.CompilerParams(vmem_limit_bytes=50 << 20),
        cost_estimate=pl.CostEstimate(flops=0, bytes_accessed=4 * length * width, transcendentals=0),
    )(embeddings)

    near = swapped(normed, devices, 1)
    across = swapped(normed, devices, 2)
    first = shifted(normed, devices, QUAD, -2 * QUAD)
    pairs = (("own", "own"), ("near", "own"))
    state, held = products(bounds, where, {"own": normed, "near": near}, pairs, keep=("near",))

    later, *state = lax.optimization_barrier((normed, *state))
    second = shifted(later, devices, -2 * QUAD, QUAD)

    across, *state = lax.optimization_barrier((across, *state))
    across_near = swapped(across, devices, 1)
    held["across"], held["first"] = across, first
    pairs = (("across", "own"), ("first", "own"), ("first", "near"), ("first", "across"))
    state, held = products(bounds, where, held, pairs, state, keep=("across", "first"))

    held["second"] = second
    pairs = (("second", "own"), ("second", "near"), ("second", "across"))
    state, held = products(bounds, where, held, pairs, state)

    held["across_near"] = across_near
    del held["near"], held["across"]
    pairs = (("across_near", "own"), ("first", "across_near"), ("second", "across_near"))
    (quad, first_best, second_best), unused = products(bounds, where, held, pairs, state, ends=True)

    received = swapped(jnp.concatenate([quad[1::2], second_best]), devices, 1)
    own_chip = jnp.maximum(quad[0::2], received[:2])
    outside = shifted(jnp.concatenate([first_best, received[2:]]), devices, -QUAD, 2 * QUAD)
    swapped_quad = swapped(own_chip[1:], devices, 2)
    even = place % 2 == 0
    landed = jnp.where(even, place + QUAD < devices, place >= 2 * QUAD)
    outside = jnp.where(landed, outside, jnp.float32(FILLER))
    swapped_outside = swapped(outside[1:], devices, 1)
    best = jnp.maximum(jnp.maximum(own_chip[:1], swapped_quad), jnp.maximum(outside[:1], swapped_outside))
    return best.reshape(length)


def solution(mesh):
    devices = 1
    for axis in AXES:
        devices *= mesh.shape[axis]
    in_specs = (P(AXES, None), P())
    return jax.shard_map(functools.partial(local, devices), mesh=mesh, in_specs=in_specs, out_specs=P(AXES), check_vma=False)
```

```python
import functools

import jax
import jax.numpy as jnp
from jax import lax
from jax.experimental import pallas as pl
from jax.experimental.pallas import tpu as pltpu
from jax.sharding import PartitionSpec as P

AXES = ("row", "col")
QUAD = 4
STRIP = 16
FILLER = -2.0
IN_QUAD = ("own", "near", "across", "across_near")
NT = (((1,), (1,)), ((), ()))


def swapped(x, devices, bit):
    return lax.ppermute(x, AXES, [(i, i ^ bit) for i in range(devices)])


def shifted(x, devices, even, odd):
    moves = [(i, i + (odd if i % 2 else even)) for i in range(devices)]
    return lax.ppermute(x, AXES, [(i, j) for i, j in moves if 0 <= j < devices])


def spans_of(bounds_ref, block, length):
    positions = block * length + lax.broadcasted_iota(jnp.int32, (1, length), 1)
    starts, ends = jnp.zeros_like(positions), jnp.full_like(positions, jnp.iinfo(jnp.int32).max)
    for c in range(bounds_ref.shape[0]):
        bound = bounds_ref[c]
        passed = bound <= positions
        starts = jnp.where(passed, jnp.maximum(starts, bound), starts)
        ends = jnp.where(passed, ends, jnp.minimum(ends, bound))
    return starts, ends


def label_at(bounds_ref, row):
    label = jnp.where(row < 0, -1, 0)
    for c in range(bounds_ref.shape[0]):
        label = label + jnp.where(bounds_ref[c] <= row, 1, 0)
    return label


def touch(bounds_ref, one, other, length):
    lower, upper = jnp.minimum(one, other), jnp.maximum(one, other)
    return label_at(bounds_ref, (lower + 1) * length - 1) == label_at(bounds_ref, upper * length)


def masked_scores(left, right, block, spans):
    scores = lax.dot_general(left[...], right[...], NT, preferred_element_type=jnp.float32)
    positions = block * left.shape[0] + lax.broadcasted_iota(jnp.int32, scores.shape, 0)
    return jnp.where((positions >= spans[0]) & (positions < spans[1]), scores, FILLER)


def folded(masked):
    result = masked[:, :128]
    for i in range(128, masked.shape[1], 128):
        result = jnp.maximum(result, masked[:, i:i + 128])
    return result


def over_rows(masked):
    return jnp.max(masked, axis=0, keepdims=True)


def normalize_kernel(raw_hbm, normed, raw, sems):
    pieces = sems.shape[0]
    length = raw.shape[0] // pieces
    copies = []
    for i in range(pieces):
        rows = pl.ds(i * length, length)
        copies.append(pltpu.make_async_copy(raw_hbm.at[rows], raw.at[rows], sems.at[i]))
    for copy in copies:
        copy.start()
    for i in range(pieces):
        copies[i].wait()
        for j in range(0, length, STRIP):
            rows = pl.ds(i * length + j, STRIP)
            widened = raw[rows, :].astype(jnp.float32)
            squares = jnp.sum(widened * widened, axis=1, keepdims=True) + 1e-06
            normed[rows, :] = (widened * lax.rsqrt(squares)).astype(jnp.bfloat16)


def products_kernel(names, pairs, keep, starts, ends, bounds_ref, place_ref, *refs):
    sources, refs = refs[:len(names)], refs[len(names):]
    if not starts:
        entering, refs = refs[:3], refs[3:]
    (quad_out, first_out, second_out), kept, refs = refs[:3], refs[3:3 + len(keep)], refs[3 + len(keep):]
    length = sources[0].shape[0]
    sources, copies = dict(zip(names, sources)), {}
    if keep:
        *refs, sems = refs
        for i, (name, ref) in enumerate(zip(keep, kept)):
            copies[name] = pltpu.make_async_copy(sources[name], ref, sems.at[i])
            copies[name].start()
            sources[name] = ref
    widest = dict(zip(("first", "second"), refs if ends else (first_out, second_out)))
    for i, ref in enumerate((quad_out, widest["first"], widest["second"])):
        ref[...] = jnp.full_like(ref, FILLER) if starts else entering[i][...]
    place = place_ref[0]
    below, above = place - QUAD, place + 2 * QUAD
    even = place % 2 == 0
    blocks = {name: place ^ b for b, name in enumerate(IN_QUAD)}
    blocks["first"], blocks["second"] = jnp.where(even, below, above), jnp.where(even, above, below)
    spans = {name: spans_of(bounds_ref, blocks[name], length) for name in {pair[1]: 0 for pair in pairs}}
    for left, right in pairs:
        for name in (left, right):
            if name in copies:
                copies.pop(name).wait()

        def multiply(left=left, right=right):
            scores = masked_scores(sources[left], sources[right], blocks[left], spans[right])
            if left == right:
                rows = lax.broadcasted_iota(jnp.int32, scores.shape, 0)
                columns = lax.broadcasted_iota(jnp.int32, scores.shape, 1)
                scores = jnp.where(rows == columns, FILLER, scores)
            b = IN_QUAD.index(right)
            quad_out[b:b + 1, :] = jnp.maximum(quad_out[b:b + 1, :], over_rows(scores))
            if left in widest:
                widest[left][...] = jnp.maximum(widest[left][...], folded(scores))
            if left == "across":
                b = IN_QUAD.index(left)
                quad_out[b:b + 1, :] = jnp.maximum(quad_out[b:b + 1, :], over_rows(folded(scores).T))

        if left == right:
            multiply()
            continue
        wanted = touch(bounds_ref, blocks[left], blocks[right], length)
        if left == "across":
            wanted &= place // 2 % 2 == ("own", "near").index(right)
        pl.when(wanted)(multiply)
    if ends:
        first_out[...] = over_rows(widest["first"][...].T)
        second_out[...] = over_rows(widest["second"][...].T)


HBM = pl.BlockSpec(memory_space=pltpu.HBM)
ANY = pl.BlockSpec(memory_space=pl.ANY)
VMEM = pl.BlockSpec(memory_space=pltpu.VMEM)
SMEM = pl.BlockSpec(memory_space=pltpu.SMEM)


def products(bounds, where, blocks, pairs, state=None, ends=False, keep=()):
    names = tuple(blocks)
    length, width = blocks[names[0]].shape
    folds = jax.ShapeDtypeStruct((length, 128), jnp.float32)
    line = jax.ShapeDtypeStruct((1, length), jnp.float32)
    block = jax.ShapeDtypeStruct((length, width), jnp.bfloat16)
    entering = () if state is None else state
    results = pl.pallas_call(
        functools.partial(products_kernel, names, pairs, keep, state is None, ends),
        out_shape=(jax.ShapeDtypeStruct((QUAD, length), jnp.float32),) + ((line, line) if ends else (folds, folds)) + (block,) * len(keep),
        in_specs=[SMEM, SMEM] + [ANY if name in keep else VMEM for name in names] + [VMEM] * len(entering),
        out_specs=(VMEM,) * (3 + len(keep)),
        scratch_shapes=[pltpu.VMEM((length, 128), jnp.float32)] * (2 if ends else 0)
        + ([pltpu.SemaphoreType.DMA((len(keep),))] if keep else []),
        compiler_params=pltpu.CompilerParams(vmem_limit_bytes=24 << 20),
        cost_estimate=pl.CostEstimate(
            flops=0,
            bytes_accessed=0,
            transcendentals=0,
        ),
    )(bounds, where, *blocks.values(), *entering)
    return results[:3], {**blocks, **dict(zip(keep, results[3:]))}


def local(devices, embeddings, cluster_sizes):
    length, width = embeddings.shape
    place = lax.axis_index(AXES).astype(jnp.int32)
    bounds = jnp.cumsum(cluster_sizes).astype(jnp.int32)
    where = place.reshape(1)

    normed = pl.pallas_call(
        normalize_kernel,
        out_shape=jax.ShapeDtypeStruct((length, width), jnp.bfloat16),
        in_specs=[HBM],
        out_specs=VMEM,
        scratch_shapes=[pltpu.VMEM((length, width), jnp.bfloat16), pltpu.SemaphoreType.DMA((4,))],
        compiler_params=pltpu.CompilerParams(vmem_limit_bytes=50 << 20),
        cost_estimate=pl.CostEstimate(flops=0, bytes_accessed=4 * length * width, transcendentals=0),
    )(embeddings)

    near = swapped(normed, devices, 1)
    across = swapped(normed, devices, 2)
    first = shifted(normed, devices, QUAD, -2 * QUAD)
    pairs = (("own", "own"), ("near", "own"))
    state, held = products(bounds, where, {"own": normed, "near": near}, pairs, keep=("near",))

    later, *state = lax.optimization_barrier((normed, *state))
    second = shifted(later, devices, -2 * QUAD, QUAD)

    across, *state = lax.optimization_barrier((across, *state))
    across_near = swapped(across, devices, 1)
    held["across"], held["first"] = across, first
    pairs = (("across", "own"), ("across", "near"), ("first", "own"), ("first", "near"), ("first", "across"))
    state, held = products(bounds, where, held, pairs, state, keep=("across", "first"))

    held["second"] = second
    pairs = (("second", "own"), ("second", "near"), ("second", "across"))
    state, held = products(bounds, where, held, pairs, state)

    held["across_near"] = across_near
    held = {name: held[name] for name in ("first", "second", "across_near")}
    pairs = (("first", "across_near"), ("second", "across_near"))
    (quad, first_best, second_best), unused = products(bounds, where, held, pairs, state, ends=True)

    received = swapped(jnp.concatenate([quad[1::2], second_best]), devices, 1)
    own_chip = jnp.maximum(quad[0::2], received[:2])
    outside = shifted(jnp.concatenate([first_best, received[2:]]), devices, -QUAD, 2 * QUAD)
    swapped_quad = swapped(own_chip[1:], devices, 2)
    even = place % 2 == 0
    landed = jnp.where(even, place + QUAD < devices, place >= 2 * QUAD)
    outside = jnp.where(landed, outside, jnp.float32(FILLER))
    swapped_outside = swapped(outside[1:], devices, 1)
    best = jnp.maximum(jnp.maximum(own_chip[:1], swapped_quad), jnp.maximum(outside[:1], swapped_outside))
    return best.reshape(length)


def solution(mesh):
    devices = 1
    for axis in AXES:
        devices *= mesh.shape[axis]
    in_specs = (P(AXES, None), P())
    return jax.shard_map(functools.partial(local, devices), mesh=mesh, in_specs=in_specs, out_specs=P(AXES), check_vma=False)
```
